256 devices in a mesh: pair: 8 (over y_hi, x), tile: 32 (over y_lo, z, core).
Axes of the slice: x: 4, y: 4 (y_hi: 2, y_lo: 2; y = y_hi * 2 + y_lo), z: 8, core: 2. Of those that a mesh axis runs over, the one named last changes fastest.
Arguments:
- amplitudes: bfloat16 [4096, 14592], P(('pair', 'tile')), may hold values from -6 to 6
- integral_tiles: bfloat16 [32, 2432, 2432], P('tile'), may hold values from -0.0546875 to 0.0546875
- tile_rows: int32 [32], replicated, may hold values from 0 to 5, as said below
- tile_cols: int32 [32], replicated, may hold values from 0 to 5, as said below
- mirror: int32 [4096], P(('pair', 'tile')), may hold values from 0 to 4095, as said below
- occupied_sum: float32 [4096], P(('pair', 'tile')), may hold values from -3 to -0.5
- virtual_sum: float32 [14592], replicated, may hold values from 0.5 to 4
Outputs:
- updated: float32 [4096, 14592], P(('pair', 'tile'))
The draws below stay inside these ranges and needn't reach their ends.
Inputs may be any that keep to these rules, and one draw needn't show every extreme that they name: Each (tile_rows[t], tile_cols[t]) occurs once, and every block number occurs in tile_rows and in tile_cols. `tile_cols`: drawn together with tile_rows. mirror is an involution without fixed points; the pairs of one device have their partners all on the one device 8 // 2 steps away along pair with the same index along tile.
All inputs are finite; a program needn't handle non-finite values.
Results may differ from the reference program's by a relative error of at most 0.0017.
Values may be sent and summed in bfloat16 or wider, within the bound.
No kernel may reach another device: no remote copies, remote signals or barrier semaphores. Data moves between devices by JAX's collectives and lax.ppermute only.
A program may use at most 192 MiB of HBM per device.

```python
import jax
import jax.numpy as jnp
from jax import lax

BLOCK = 2432
NBLOCKS = 6
PAIR_DEV = 512
PAIRS = 4096
NTILES = 32
WIDTH = 14592
N_PAIR = 8
N_TILE = 32


def tile_map(key):
    base = jax.random.fold_in(key, 11)
    cells = jnp.arange(NBLOCKS * NBLOCKS, dtype=jnp.int32)
    offset = jax.random.randint(jax.random.fold_in(base, 1), (), 0, NBLOCKS)
    band = (cells % NBLOCKS - cells // NBLOCKS - offset) % NBLOCKS == 0
    ranks = jax.random.permutation(jax.random.fold_in(base, 2), NBLOCKS * NBLOCKS).astype(jnp.int32)
    score = ranks + jnp.where(band, 0, NBLOCKS * NBLOCKS).astype(jnp.int32)
    chosen = jnp.argsort(score, stable=True)[:NTILES].astype(jnp.int32)
    order = jax.random.permutation(jax.random.fold_in(base, 3), NTILES)
    chosen = chosen[order]
    return ((chosen // NBLOCKS).astype(jnp.int32), (chosen % NBLOCKS).astype(jnp.int32))


def draw_tile_rows(key, part):
    return tile_map(key)[0]


def draw_tile_cols(key, part):
    return tile_map(key)[1]


def draw_mirror(key, part):
    half = N_PAIR // 2
    local_rows = PAIR_DEV // N_TILE
    keys = jax.random.split(jax.random.fold_in(key, 5), half * N_TILE)
    sigma = jax.vmap(lambda single: jax.random.permutation(single, local_rows))(keys)
    sigma = sigma.reshape(half, N_TILE, local_rows).astype(jnp.int32)
    inverse = jnp.argsort(sigma, axis=-1, stable=True).astype(jnp.int32)
    lower = jnp.arange(half, dtype=jnp.int32)[:, None, None]
    column = jnp.arange(N_TILE, dtype=jnp.int32)[None, :, None]
    first = ((lower + half) * N_TILE + column) * local_rows + sigma
    second = (lower * N_TILE + column) * local_rows + inverse
    return jnp.concatenate([first, second], axis=0).reshape(-1).astype(jnp.int32)


def shard_levels(rng, shape, cuts, low, largest):
    def one(axis_at, blocks):
        draws = jax.random.uniform(jax.random.fold_in(jax.random.fold_in(rng, 6), axis_at), (blocks,), jnp.float32, low / len(cuts), largest / len(cuts))
        return jnp.repeat(jnp.exp(draws), shape[axis_at] // blocks).reshape((-1,) + (1,) * (len(shape) - axis_at - 1))

    gain = one(*cuts[0])
    for cut in cuts[1:]:
        gain = gain * one(*cut)
    return gain


def bell_draw(own_key, extent, deviation, reach, pieces=(), kind=jnp.bfloat16):
    values = jax.random.normal(own_key, extent, jnp.float32) * deviation
    if len(pieces) > 0:
        values = shard_levels(own_key, extent, pieces, -0.22, 0.18) * values
    return jnp.clip(values, min=-reach, max=reach).astype(kind)


def setup_inputs(seed: int = 0) -> dict:
    key_of = jax.random.split(jax.random.key(seed), 8)
    amplitudes = bell_draw(key_of[0], (PAIRS, WIDTH), 1.0, 6.0, ((0, 256),))
    integral_tiles = bell_draw(key_of[1], (NTILES, BLOCK, BLOCK), (BLOCK * NTILES // NBLOCKS) ** -0.5, 0.0546875, ((0, 32),))
    tile_rows = draw_tile_rows(jax.random.fold_in(key_of[7], 71), 0)
    tile_cols = draw_tile_cols(jax.random.fold_in(key_of[7], 71), 0)
    mirror = draw_mirror(jax.random.fold_in(key_of[7], 71), 0)
    occupied_sum = jnp.clip(-3.0 + 2.5 * jax.random.uniform(key_of[5], (PAIRS,), jnp.float32) ** shard_levels(key_of[5], (PAIRS,), ((0, 256),), -0.2, 0.2), -3.0, -0.5)
    virtual_sum = jnp.clip(jax.random.uniform(key_of[6], (WIDTH,), jnp.float32, 0.5, 4.0), 0.5, 4.0)
    return {"amplitudes": amplitudes, "integral_tiles": integral_tiles, "tile_rows": tile_rows, "tile_cols": tile_cols, "mirror": mirror, "occupied_sum": occupied_sum, "virtual_sum": virtual_sum}


def reference(amplitudes, integral_tiles, tile_rows, tile_cols, mirror, occupied_sum, virtual_sum):
    blocked = amplitudes.reshape(PAIRS, NBLOCKS, BLOCK)

    def add_tile(total, item):
        tile, row_block, col_block = item
        picked = lax.dynamic_index_in_dim(blocked, col_block.astype(jnp.int32), 1, keepdims=False)
        term = jnp.dot(picked, tile.T, preferred_element_type=jnp.float32)
        current = lax.dynamic_index_in_dim(total, row_block.astype(jnp.int32), 1, keepdims=False)
        total = lax.dynamic_update_index_in_dim(total, current + term, row_block.astype(jnp.int32), 1)
        return total, None

    start = jnp.zeros((PAIRS, NBLOCKS, BLOCK), jnp.float32)
    residual, unused = lax.scan(add_tile, start, (integral_tiles, tile_rows, tile_cols))
    residual = residual.reshape(PAIRS, WIDTH)
    combined = residual - 0.5 * residual[mirror]
    denominator = virtual_sum[None, :] - occupied_sum[:, None]
    return amplitudes.astype(jnp.float32) + combined / denominator
```

```python
import jax
import jax.numpy as jnp
from jax import lax
from jax.experimental import pallas as pl
from jax.experimental.pallas import tpu as pltpu
from jax.sharding import PartitionSpec as P

BOTH = ("pair", "tile")
SCALE = 8.0


def moved(dx=0, dy=0, dz=0, core=0):
    pairs = []
    for x in range(4):
        for y in range(4):
            for z in range(8):
                for c in range(2):
                    far_y = (y + dy) % 4
                    here = ((y // 2) * 4 + x) * 32 + (y % 2) * 16 + z * 2 + c
                    there = (
                        ((far_y // 2) * 4 + (x + dx) % 4) * 32
                        + (far_y % 2) * 16
                        + ((z + dz) % 8) * 2
                        + (c ^ core)
                    )
                    pairs.append((here, there))
    return pairs


def send(array, **by):
    return lax.ppermute(array, BOTH, moved(**by))


def terms_kernel(rows_ref, tile_ref, out_ref):
    out_ref[...] = SCALE * lax.dot_general(
        rows_ref[...], tile_ref[...], (((1,), (1,)), ((), ())), preferred_element_type=jnp.float32
    )


def tile_terms(rows, tile):
    count, width = rows.shape
    step = 512
    return pl.pallas_call(
        terms_kernel,
        out_shape=jax.ShapeDtypeStruct((count, width), jnp.float32),
        grid=(pl.cdiv(width, step),),
        in_specs=[
            pl.BlockSpec((count, width), lambda i: (0, 0)),
            pl.BlockSpec((step, width), lambda i: (i, 0)),
        ],
        out_specs=pl.BlockSpec((count, step), lambda i: (0, i)),
        cost_estimate=pl.CostEstimate(
            flops=2 * count * width * width, bytes_accessed=2 * width * width, transcendentals=0
        ),
        compiler_params=pltpu.CompilerParams(vmem_limit_bytes=32 * 1024 * 1024),
    )(rows, tile)


def local(amplitudes, integral_tiles, tile_rows, tile_cols, mirror, occupied_sum, virtual_sum):
    local_rows, total_width = amplitudes.shape
    width = integral_tiles.shape[1]
    blocks = total_width // width
    half = local_rows // 2
    rows = 8 * half
    here = lax.axis_index("tile")
    plane = (here, here ^ 1, here ^ 16, here ^ 17)
    cols = [tile_cols[t] for t in plane]
    outs = [tile_rows[t] for t in plane]

    blocked = amplitudes.reshape(local_rows, blocks, width).transpose(1, 0, 2)
    halves = [blocked[:, :half], blocked[:, half:]]
    pieces = [[None] * 8, [None] * 8]
    pieces[0][0], pieces[1][0] = halves
    up, down = list(halves), list(halves)
    for hop in range(1, 5):
        for h, ahead in ((0, True), (1, False), (1, True), (0, False)):
            if hop == 4 and ahead == (h == 1):
                continue
            if ahead:
                up[h] = send(up[h], dz=1)
                pieces[h][-hop % 8] = up[h]
            else:
                down[h] = send(down[h], dz=-1)
                pieces[h][hop] = down[h]

    def pick(h, col):
        return jnp.concatenate(
            [lax.dynamic_index_in_dim(p, col, 0, keepdims=False) for p in pieces[h]], axis=0
        )

    from_below = send(jnp.stack([pick(0, cols[2]), pick(0, cols[3])]), dy=1)
    from_above = send(jnp.stack([pick(1, cols[2]), pick(1, cols[3])]), dy=-1)
    to_core = jnp.concatenate([pick(0, cols[1]), pick(1, cols[1]), from_below[1], from_above[1]], axis=0)
    from_core = send(to_core, core=1)
    stacked = jnp.concatenate(
        [pick(0, cols[0]), pick(1, cols[0]), from_below[0], from_above[0], from_core], axis=0
    )
    terms = tile_terms(stacked, integral_tiles[0]).astype(jnp.float16)
    mine, theirs = terms[: 4 * rows], terms[4 * rows :]
    other = send(theirs, core=1)
    below = jnp.stack([mine[2 * rows : 3 * rows], other[2 * rows : 3 * rows]])
    above = jnp.stack([mine[3 * rows :], other[3 * rows :]])
    back = [send(below, dy=-1), send(above, dy=1)]

    def contribution(h, delta):
        at = slice(delta * half, (delta + 1) * half)
        four = [
            mine[h * rows : (h + 1) * rows][at],
            other[h * rows : (h + 1) * rows][at],
            back[h][0][at],
            back[h][1][at],
        ]
        four = [f.astype(jnp.float32) for f in four]
        return jnp.stack(
            [
                sum(jnp.where(out == k, f, 0.0) for out, f in zip(outs, four))
                for k in range(blocks)
            ]
        )

    down_sum = [contribution(0, 4), contribution(1, 5)]
    up_sum = [contribution(0, 3), contribution(1, 4)]
    down_at, up_at = [4, 5], [3, 4]
    for hop in range(4, 0, -1):
        for h, ahead in ((0, False), (1, True), (1, False), (0, True)):
            sums, at = (up_sum, up_at) if ahead else (down_sum, down_at)
            if (at[h] if ahead else 8 - at[h]) != hop:
                continue
            arrived = send(sums[h].astype(jnp.float16), dz=1 if ahead else -1).astype(jnp.float32)
            at[h] = at[h] - 1 if ahead else (at[h] + 1) % 8
            sums[h] = arrived + contribution(h, at[h]) if at[h] else arrived
    residual = jnp.concatenate(
        [up_sum[h] + down_sum[h] + contribution(h, 0) for h in range(2)], axis=1
    ) * (1.0 / SCALE)
    residual = residual.transpose(1, 0, 2).reshape(local_rows, total_width)
    partner_rows = send(residual.astype(jnp.bfloat16), dy=2).astype(residual.dtype)
    partner_index = mirror % local_rows
    combined = residual - 0.5 * partner_rows[partner_index]
    denominator = virtual_sum[None, :] - occupied_sum[:, None]
    return amplitudes.astype(jnp.float32) + combined / denominator


def solution(mesh):
    in_specs = (
        P(("pair", "tile"), None),
        P("tile", None, None),
        P(),
        P(),
        P(("pair", "tile")),
        P(("pair", "tile")),
        P(),
    )
    out_specs = P(("pair", "tile"), None)
    return jax.shard_map(local, mesh=mesh, in_specs=in_specs, out_specs=out_specs, check_vma=False)
```

```python
import functools

import jax
import jax.numpy as jnp
from jax import lax
from jax.experimental import pallas as pl
from jax.experimental.pallas import tpu as pltpu
from jax.sharding import PartitionSpec as P

BOTH = ("pair", "tile")
SCALE = 8.0


def moved(dx=0, dy=0, dz=0, core=0):
    pairs = []
    for x in range(4):
        for y in range(4):
            for z in range(8):
                for c in range(2):
                    far_y = (y + dy) % 4
                    here = ((y // 2) * 4 + x) * 32 + (y % 2) * 16 + z * 2 + c
                    there = (
                        ((far_y // 2) * 4 + (x + dx) % 4) * 32
                        + (far_y % 2) * 16
                        + ((z + dz) % 8) * 2
                        + (c ^ core)
                    )
                    pairs.append((here, there))
    return pairs


def send(array, **by):
    return lax.ppermute(array, BOTH, moved(**by))


def tied(*arrays):
    return lax.optimization_barrier(arrays)


def vmem():
    return pl.BlockSpec(memory_space=pltpu.VMEM)


def pick_kernel(count, cols_ref, *refs):
    low, high = refs[:count], refs[count : 2 * count]
    up_ref, down_ref, own_ref, cross_ref = refs[2 * count :]
    here = lax.axis_index("tile")
    mine, core, far, far_core = [cols_ref[here ^ bit] for bit in (0, 1, 16, 17)]
    for i in range(count):
        own_ref[0, i] = low[i][mine]
        own_ref[1, i] = high[i][mine]
        cross_ref[0, i] = low[i][core]
        cross_ref[1, i] = high[i][core]
        up_ref[0, i] = low[i][far]
        up_ref[1, i] = low[i][far_core]
        down_ref[0, i] = high[i][far]
        down_ref[1, i] = high[i][far_core]


def picks(low, high, cols):
    count = len(low)
    half, width = low[0].shape[1:]
    out = jax.ShapeDtypeStruct((2, count, half, width), low[0].dtype)
    return pl.pallas_call(
        functools.partial(pick_kernel, count),
        out_shape=[out] * 4,
        in_specs=[pl.BlockSpec(memory_space=pltpu.SMEM)] + [vmem()] * (2 * count),
        out_specs=[vmem()] * 4,
        cost_estimate=pl.CostEstimate(
            flops=0, bytes_accessed=16 * count * half * width, transcendentals=0
        ),
        compiler_params=pltpu.CompilerParams(vmem_limit_bytes=24 * 1024 * 1024),
    )(cols, *low, *high)


STEP = 512


def terms_kernel(rows_ref, tile_ref, out_ref, held, sems):
    width = tile_ref.shape[0]
    parts = [slice(start, min(start + STEP, width)) for start in range(0, width, STEP)]
    copies = [
        pltpu.make_async_copy(tile_ref.at[part], held.at[part], sems.at[i])
        for i, part in enumerate(parts)
    ]
    for copy in copies[:2]:
        copy.start()
    for i, (part, copy) in enumerate(zip(parts, copies)):
        copy.wait()
        if i + 2 < len(copies):
            copies[i + 2].start()
        out_ref[:, part] = SCALE * lax.dot_general(
            rows_ref[...], held[part, :], (((1,), (1,)), ((), ())), preferred_element_type=jnp.float32
        )


def tile_terms(rows, tile):
    count, width = rows.shape
    return pl.pallas_call(
        terms_kernel,
        out_shape=jax.ShapeDtypeStruct((count, width), jnp.float32),
        in_specs=[vmem(), pl.BlockSpec(memory_space=pltpu.HBM)],
        out_specs=vmem(),
        scratch_shapes=[
            pltpu.VMEM(tile.shape, tile.dtype),
            pltpu.SemaphoreType.DMA((pl.cdiv(width, STEP),)),
        ],
        cost_estimate=pl.CostEstimate(
            flops=2 * count * width * width, bytes_accessed=2 * width * width, transcendentals=0
        ),
        compiler_params=pltpu.CompilerParams(vmem_limit_bytes=44 * 1024 * 1024),
    )(rows, tile)


GROUPS = ((0, 1, 7, 2, 6), (3, 5, 4))


def local(amplitudes, integral_tiles, tile_rows, tile_cols, mirror, occupied_sum, virtual_sum):
    local_rows, total_width = amplitudes.shape
    width = integral_tiles.shape[1]
    blocks = total_width // width
    half = local_rows // 2
    here = lax.axis_index("tile")
    plane = jnp.stack([here, here ^ 1, here ^ 16, here ^ 17])
    named = plane[:, None] == jnp.arange(tile_rows.shape[0], dtype=jnp.int32)[None, :]
    outs = jnp.sum(jnp.where(named, tile_rows[None, :], 0), axis=1)
    hits = outs[None, :] == jnp.arange(blocks, dtype=jnp.int32)[:, None]
    hits = hits.astype(jnp.float32)

    blocked = amplitudes.reshape(local_rows, blocks, width).transpose(1, 0, 2)
    halves = [blocked[:, :half], blocked[:, half:]]
    pieces = [[None] * 8, [None] * 8]
    pieces[0][0], pieces[1][0] = halves
    long = halves
    short = [halves[1], halves[0]]
    for hop in range(1, 5):
        long = tied(send(long[0], dz=1), send(long[1], dz=-1))
        pieces[0][-hop % 8], pieces[1][hop] = long
        if hop < 4:
            short = tied(send(short[0], dz=1), send(short[1], dz=-1))
            pieces[1][-hop % 8], pieces[0][hop] = short

    tile = integral_tiles[0]

    def collected(group):
        return [pieces[h][d] for h in range(2) for d in group]

    def out_by_y(pieces_of, group):
        count = len(group)
        rows = count * half
        to_up, to_down, own, cross = picks(pieces_of[:count], pieces_of[count:], tile_cols)
        to_up, to_down = [a.reshape(2, rows, width) for a in (to_up, to_down)]
        own, cross = [a.reshape(2 * rows, width) for a in (own, cross)]
        return own, cross, send(to_up, dy=1), send(to_down, dy=-1)

    near, far = GROUPS
    moved_parts = [out_by_y(collected(group), group) for group in GROUPS]
    own = jnp.concatenate(
        [part[0] for part in moved_parts]
        + [arrived[0] for part in moved_parts for arrived in part[2:]],
        axis=0,
    )
    cross = jnp.concatenate(
        [part[1] for part in moved_parts]
        + [arrived[1] for part in moved_parts for arrived in part[2:]],
        axis=0,
    )
    stacked = jnp.concatenate([own, send(cross, core=1)], axis=0)
    terms = tile_terms(stacked, tile).astype(jnp.float16)
    mine, theirs = jnp.split(terms, 2)
    other = send(theirs, core=1)

    starts = {}
    at = 0
    for kind in ("own", "moved"):
        for group in GROUPS:
            for h in range(2):
                starts[kind, group, h] = at
                at += len(group) * half

    def rows_of(array, kind, group, h):
        at = starts[kind, group, h]
        return array[at : at + len(group) * half]

    def back_by_y(group):
        below, above = [
            jnp.stack([rows_of(array, "moved", group, h) for array in (mine, other)])
            for h in range(2)
        ]
        return send(below, dy=-1), send(above, dy=1)

    far_back = back_by_y(far)
    near_back = back_by_y(near)

    def split(group, back):
        four = {}
        for h in range(2):
            parts = [rows_of(array, "own", group, h) for array in (mine, other)]
            parts += [back[h][0], back[h][1]]
            for i, delta in enumerate(group):
                four[h, delta] = [part[i * half : (i + 1) * half] for part in parts]
        return four

    def planes(group, back):
        four = split(group, back)
        keys = list(four)
        totals = []
        for key in keys:
            total = sum(
                hits[:, i][:, None, None] * f.astype(jnp.float32)[None]
                for i, f in enumerate(four[key])
            )
            totals.append(total.reshape(blocks * half, width))
        return dict(zip(keys, tied(*totals)))

    dense = planes(far, far_back)

    def passed_on(below, above):
        below, above = [a.astype(jnp.float16) for a in (below, above)]
        arrived = tied(send(below, dz=-1), send(above, dz=1))
        return [a.astype(jnp.float32) for a in arrived]

    short = [dense[1, 5], dense[0, 3]]
    long = [dense[0, 4], dense[1, 4]]
    for hop in range(4, 0, -1):
        if hop < 4:
            long = [long[0] + dense[0, 8 - hop], long[1] + dense[1, hop]]
        long = passed_on(*long)
        if hop == 4:
            *near_back, long[0], long[1] = tied(*near_back, *long)
            dense.update(planes(near, near_back))
        if hop < 4:
            if hop < 3:
                short = [short[0] + dense[1, 8 - hop], short[1] + dense[0, hop]]
            short = passed_on(*short)
    sums = [long[0] + short[1], long[1] + short[0]]
    residual = jnp.concatenate(
        [(sums[h] + dense[h, 0]).reshape(blocks, half, width) for h in range(2)], axis=1
    ) * (1.0 / SCALE)
    residual = residual.transpose(1, 0, 2).reshape(local_rows, total_width)
    partner_rows = send(residual.astype(jnp.bfloat16), dy=2).astype(residual.dtype)
    partner_index = mirror % local_rows
    combined = residual - 0.5 * partner_rows[partner_index]
    denominator = virtual_sum[None, :] - occupied_sum[:, None]
    return amplitudes.astype(jnp.float32) + combined / denominator


def solution(mesh):
    in_specs = (
        P(("pair", "tile"), None),
        P("tile", None, None),
        P(),
        P(),
        P(("pair", "tile")),
        P(("pair", "tile")),
        P(),
    )
    out_specs = P(("pair", "tile"), None)
    return jax.shard_map(local, mesh=mesh, in_specs=in_specs, out_specs=out_specs, check_vma=False)
```

```python
import functools

import jax
import jax.numpy as jnp
from jax import lax
from jax.experimental import pallas as pl
from jax.experimental.pallas import tpu as pltpu
from jax.sharding import PartitionSpec as P

BOTH = ("pair", "tile")
SCALE = 8.0


def moved(dx=0, dy=0, dz=0, core=0):
    pairs = []
    for x in range(4):
        for y in range(4):
            for z in range(8):
                for c in range(2):
                    far_y = (y + dy) % 4
                    here = ((y // 2) * 4 + x) * 32 + (y % 2) * 16 + z * 2 + c
                    there = (
                        ((far_y // 2) * 4 + (x + dx) % 4) * 32
                        + (far_y % 2) * 16
                        + ((z + dz) % 8) * 2
                        + (c ^ core)
                    )
                    pairs.append((here, there))
    return pairs


def send(array, **by):
    return lax.ppermute(array, BOTH, moved(**by))


def tied(*arrays):
    return lax.optimization_barrier(arrays)


def vmem():
    return pl.BlockSpec(memory_space=pltpu.VMEM)


def call(kernel, outs, operands, smem=0, scratch=(), flops=0, moved=None, far=0, limit=24):
    if moved is None:
        moved = sum(2 * out.size * out.dtype.itemsize for out in outs)
    specs = [pl.BlockSpec(memory_space=pltpu.SMEM)] * smem + [vmem()] * (len(operands) - smem - far)
    specs += [pl.BlockSpec(memory_space=pltpu.HBM)] * far
    return pl.pallas_call(
        kernel,
        out_shape=list(outs),
        in_specs=specs,
        out_specs=[vmem()] * len(outs),
        scratch_shapes=list(scratch),
        cost_estimate=pl.CostEstimate(flops=flops, bytes_accessed=moved, transcendentals=0),
        compiler_params=pltpu.CompilerParams(vmem_limit_bytes=limit * 1024 * 1024),
    )(*operands)


BITS = (0, 1, 16, 17)


def at_plane(here, dz):
    return (here & 17) | ((((here >> 1) + dz) & 7) << 1)


def pick_kernel(count, cols_ref, *refs):
    low, high = refs[:count], refs[count : 2 * count]
    own_ref, cross_ref, up_ref, down_ref = refs[2 * count :]
    here = lax.axis_index("tile")
    mine, core, far, far_core = [cols_ref[here ^ bit] for bit in BITS]
    for i in range(count):
        own_ref[0, i] = low[i][mine]
        own_ref[1, i] = high[i][mine]
        cross_ref[0, i] = low[i][core]
        cross_ref[1, i] = high[i][core]
        up_ref[0, i] = low[i][far]
        up_ref[1, i] = low[i][far_core]
        down_ref[0, i] = high[i][far]
        down_ref[1, i] = high[i][far_core]


def trim_kernel(cols_ref, up_ref, down_ref, to_up_ref, to_down_ref):
    here = lax.axis_index("tile")
    for dz, source, target in ((1, up_ref, to_up_ref), (-1, down_ref, to_down_ref)):
        for j, bit in enumerate(BITS):
            target[j] = source[cols_ref[at_plane(here, dz) ^ bit]]


def far_kernel(cols_ref, *refs):
    low, high = refs[:3], refs[3:6]
    own_ref, cross_ref, up_ref, down_ref = refs[6:]
    here = lax.axis_index("tile")
    for i in range(3):
        four = [cols_ref[here ^ bit] for bit in BITS] if i == 0 else range(4)
        own_ref[0, i] = low[i][four[0]]
        own_ref[1, i] = high[i][four[0]]
        cross_ref[0, i] = low[i][four[1]]
        cross_ref[1, i] = high[i][four[1]]
        for s in range(2):
            up_ref[s, i] = low[i][four[2 + s]]
            down_ref[s, i] = high[i][four[2 + s]]


def stack_kernel(*refs):
    *parts, out_ref = refs
    at = 0
    for part in parts:
        value = part[...] if len(part.shape) == 2 else part[1]
        out_ref[at : at + value.shape[0]] = value
        at += value.shape[0]


def terms_kernel(*refs):
    *parts, tile_ref, out_ref, rows_ref, held, sems = refs
    width = tile_ref.shape[0]
    slices = [slice(start, min(start + STEP, width)) for start in range(0, width, STEP)]
    copies = [
        pltpu.make_async_copy(tile_ref.at[part], held.at[part], sems.at[i])
        for i, part in enumerate(slices)
    ]
    for copy in copies[:2]:
        copy.start()
    at = 0
    for part in parts:
        value = part[...] if len(part.shape) == 2 else part[0]
        rows_ref[at : at + value.shape[0]] = value
        at += value.shape[0]
    for i, (part, copy) in enumerate(zip(slices, copies)):
        copy.wait()
        if i + 2 < len(copies):
            copies[i + 2].start()
        out_ref[:, part] = SCALE * lax.dot_general(
            rows_ref[...], held[part, :], (((1,), (1,)), ((), ())), preferred_element_type=jnp.float32
        )


STEP = 512
NEAR = ((0, 1, 7, 2, 6), (0, 1, 7, 2, 6))
FAR = ((5, 3, 4), (3, 5, 4))


def local(amplitudes, integral_tiles, tile_rows, tile_cols, mirror, occupied_sum, virtual_sum):
    local_rows, total_width = amplitudes.shape
    width = integral_tiles.shape[1]
    blocks = total_width // width
    half = local_rows // 2
    kind = amplitudes.dtype
    here = lax.axis_index("tile")

    def hits_at(dz):
        plane = jnp.stack([at_plane(here, dz) ^ bit for bit in BITS])
        named = plane[:, None] == jnp.arange(tile_rows.shape[0], dtype=jnp.int32)[None, :]
        outs = jnp.sum(jnp.where(named, tile_rows[None, :], 0), axis=1)
        hits = outs[None, :] == jnp.arange(blocks, dtype=jnp.int32)[:, None]
        return hits.astype(jnp.float32)

    def spread(hits, four):
        total = sum(
            hits[:, i][:, None, None] * f.astype(jnp.float32)[None] for i, f in enumerate(four)
        )
        return total.reshape(blocks * half, width)

    def shape(*dims):
        return jax.ShapeDtypeStruct((*dims, width), kind)

    def trimmed(up, down):
        return call(trim_kernel, [shape(4, half)] * 2, (tile_cols, up, down), smem=1)

    blocked = amplitudes.reshape(local_rows, blocks, width).transpose(1, 0, 2)
    halves = [blocked[:, :half], blocked[:, half:]]
    pieces = [[None] * 8, [None] * 8]
    pieces[0][0], pieces[1][0] = halves

    def gathered(up, down):
        size = up.shape
        flat = [a.reshape(size[0] * size[1], width) for a in (up, down)]
        arrived = tied(send(flat[0], dz=1), send(flat[1], dz=-1))
        return [a.reshape(size) for a in arrived]

    long = halves
    short = [halves[1], halves[0]]
    for hop in range(1, 5):
        long = gathered(*(long if hop < 4 else trimmed(*long)))
        pieces[0][-hop % 8], pieces[1][hop] = long
        if hop < 4:
            short = gathered(*(short if hop < 3 else trimmed(*short)))
            pieces[1][-hop % 8], pieces[0][hop] = short

    def collected(deltas):
        return [pieces[h][d] for h in range(2) for d in deltas[h]]

    def crossed(parts):
        own, cross, up, down = [a.reshape(2, -1, width) for a in parts]
        own, cross = [a.reshape(-1, width) for a in (own, cross)]
        return own, cross, send(up, dy=1), send(down, dy=-1)

    count = len(NEAR[0])
    near = crossed(
        call(
            functools.partial(pick_kernel, count),
            [shape(2, count, half)] * 4,
            (tile_cols, *collected(NEAR)),
            smem=1,
        )
    )
    far = crossed(call(far_kernel, [shape(2, 3, half)] * 4, (tile_cols, *collected(FAR)), smem=1))
    sides = (*near[2:], *far[2:])
    per_core = local_rows * 16
    (to_core,) = call(stack_kernel, [shape(per_core)], (near[1], far[1], *sides))
    (terms,) = call(
        terms_kernel,
        [jax.ShapeDtypeStruct((2 * per_core, width), jnp.float32)],
        (near[0], far[0], *sides, send(to_core, core=1), integral_tiles[0]),
        scratch=[
            pltpu.VMEM((2 * per_core, width), kind),
            pltpu.VMEM((width, width), kind),
            pltpu.SemaphoreType.DMA((pl.cdiv(width, STEP),)),
        ],
        far=1,
        limit=44,
        flops=4 * per_core * width * width,
        moved=2 * width * width,
    )
    mine, theirs = jnp.split(terms.astype(jnp.float16), 2)
    other = send(theirs, core=1)

    def back_by_y(at, size):
        below, above = [
            jnp.stack([array[start : start + size] for array in (mine, other)])
            for start in (at, at + size)
        ]
        return send(below, dy=-1), send(above, dy=1)

    near_size, far_size = count * half, 3 * half
    sides_at = 2 * (near_size + far_size)
    far_back = back_by_y(sides_at + 2 * near_size, far_size)
    near_back = back_by_y(sides_at, near_size)

    def planes(deltas, at, back):
        four = {}
        for h in range(2):
            size = len(deltas[h]) * half
            parts = [array[at + h * size : at + (h + 1) * size] for array in (mine, other)]
            parts += [back[h][0], back[h][1]]
            for i, delta in enumerate(deltas[h]):
                four[h, delta] = [part[i * half : (i + 1) * half] for part in parts]
        return four

    four = planes(FAR, 2 * near_size, far_back)
    raw = {
        key: jnp.concatenate(four.pop(key), axis=0) for key in ((0, 4), (1, 4), (1, 5), (0, 3))
    }
    above_hits, my_hits, below_hits = [hits_at(dz) for dz in (1, 0, -1)]

    def passed_on(below, above):
        below, above = [a.astype(jnp.float16) for a in (below, above)]
        return tied(send(below, dz=-1), send(above, dz=1))

    def first_hop(below, above):
        arrived = passed_on(below, above)
        return [
            spread(hits, jnp.split(a, 4)) for hits, a in zip((above_hits, below_hits), arrived)
        ]

    def hop_on(below, above):
        return [a.astype(jnp.float32) for a in passed_on(below, above)]

    long = first_hop(raw[0, 4], raw[1, 4])
    short = first_hop(raw[1, 5], raw[0, 3])
    dense = dict(zip(four, tied(*[spread(my_hits, f) for f in four.values()])))
    *near_back, long[0], long[1] = tied(*near_back, *long)
    four = planes(NEAR, 0, near_back)
    dense.update(zip(four, tied(*[spread(my_hits, f) for f in four.values()])))
    for hop in range(3, 0, -1):
        long = hop_on(long[0] + dense[0, 8 - hop], long[1] + dense[1, hop])
        if hop < 3:
            short = hop_on(short[0] + dense[1, 8 - hop], short[1] + dense[0, hop])
    sums = [long[0] + short[1], long[1] + short[0]]
    residual = jnp.concatenate(
        [(sums[h] + dense[h, 0]).reshape(blocks, half, width) for h in range(2)], axis=1
    ) * (1.0 / SCALE)
    residual = residual.transpose(1, 0, 2).reshape(local_rows, total_width)
    partner_rows = send(residual.astype(jnp.bfloat16), dy=2).astype(residual.dtype)
    partner_index = mirror % local_rows
    combined = residual - 0.5 * partner_rows[partner_index]
    denominator = virtual_sum[None, :] - occupied_sum[:, None]
    return amplitudes.astype(jnp.float32) + combined / denominator


def solution(mesh):
    in_specs = (
        P(("pair", "tile"), None),
        P("tile", None, None),
        P(),
        P(),
        P(("pair", "tile")),
        P(("pair", "tile")),
        P(),
    )
    out_specs = P(("pair", "tile"), None)
    return jax.shard_map(local, mesh=mesh, in_specs=in_specs, out_specs=out_specs, check_vma=False)
```

```python
import functools

import jax
import jax.numpy as jnp
from jax import lax
from jax.experimental import pallas as pl
from jax.experimental.pallas import tpu as pltpu
from jax.sharding import PartitionSpec as P

BOTH = ("pair", "tile")
SCALE = 8.0


def moved(dx=0, dy=0, dz=0, core=0):
    pairs = []
    for x in range(4):
        for y in range(4):
            for z in range(8):
                for c in range(2):
                    far_y = (y + dy) % 4
                    here = ((y // 2) * 4 + x) * 32 + (y % 2) * 16 + z * 2 + c
                    there = (
                        ((far_y // 2) * 4 + (x + dx) % 4) * 32
                        + (far_y % 2) * 16
                        + ((z + dz) % 8) * 2
                        + (c ^ core)
                    )
                    pairs.append((here, there))
    return pairs


def send(array, **by):
    return lax.ppermute(array, BOTH, moved(**by))


def tied(*arrays):
    return lax.optimization_barrier(arrays)


def vmem():
    return pl.BlockSpec(memory_space=pltpu.VMEM)


def call(kernel, outs, operands, smem=0, scratch=(), flops=0, moved=None, far=0, limit=24):
    if moved is None:
        moved = sum(2 * out.size * out.dtype.itemsize for out in outs)
    specs = [pl.BlockSpec(memory_space=pltpu.SMEM)] * smem + [vmem()] * (len(operands) - smem - far)
    specs += [pl.BlockSpec(memory_space=pltpu.HBM)] * far
    return pl.pallas_call(
        kernel,
        out_shape=list(outs),
        in_specs=specs,
        out_specs=[vmem()] * len(outs),
        scratch_shapes=list(scratch),
        cost_estimate=pl.CostEstimate(flops=flops, bytes_accessed=moved, transcendentals=0),
        compiler_params=pltpu.CompilerParams(vmem_limit_bytes=limit * 1024 * 1024),
    )(*operands)


BITS = (0, 1, 16, 17)


def at_plane(here, dz):
    return (here & 17) | ((((here >> 1) + dz) & 7) << 1)


def pick_kernel(count, cols_ref, *refs):
    low, high = refs[:count], refs[count : 2 * count]
    own_ref, cross_ref, up_ref, down_ref = refs[2 * count :]
    here = lax.axis_index("tile")
    mine, core, far, far_core = [cols_ref[here ^ bit] for bit in BITS]
    for i in range(count):
        own_ref[0, i] = low[i][mine]
        own_ref[1, i] = high[i][mine]
        cross_ref[0, i] = low[i][core]
        cross_ref[1, i] = high[i][core]
        up_ref[0, i] = low[i][far]
        up_ref[1, i] = low[i][far_core]
        down_ref[0, i] = high[i][far]
        down_ref[1, i] = high[i][far_core]


def trim_kernel(cols_ref, up_ref, down_ref, to_up_ref, to_down_ref):
    here = lax.axis_index("tile")
    for dz, source, target in ((1, up_ref, to_up_ref), (-1, down_ref, to_down_ref)):
        for j, bit in enumerate(BITS):
            target[j] = source[cols_ref[at_plane(here, dz) ^ bit]]


def far_kernel(cols_ref, *refs):
    low, high = refs[:3], refs[3:6]
    own_ref, cross_ref, up_ref, down_ref = refs[6:]
    here = lax.axis_index("tile")
    for i in range(3):
        four = [cols_ref[here ^ bit] for bit in BITS] if i == 0 else range(4)
        own_ref[0, i] = low[i][four[0]]
        own_ref[1, i] = high[i][four[0]]
        cross_ref[0, i] = low[i][four[1]]
        cross_ref[1, i] = high[i][four[1]]
        for s in range(2):
            up_ref[s, i] = low[i][four[2 + s]]
            down_ref[s, i] = high[i][four[2 + s]]


def gather_rows(parts, side, rows_ref):
    at = 0
    for part in parts:
        value = part[...] if len(part.shape) == 2 else part[side]
        rows_ref[at : at + value.shape[0]] = value
        at += value.shape[0]


def terms_kernel(*refs):
    parts, tiles = refs[:8], refs[8:10]
    outs, row_sets, held, sems = refs[10:12], refs[12:14], refs[14], refs[15]
    width = tiles[0].shape[0]
    steps = []
    for side in range(2):
        for start in range(0, width, STEP):
            part = slice(start, min(start + STEP, width))
            copy = pltpu.make_async_copy(
                tiles[side].at[part], held.at[side, part], sems.at[len(steps)]
            )
            steps.append((side, part, copy))
    for _, _, copy in steps[:2]:
        copy.start()
    gather_rows((parts[0], parts[1], *parts[4:]), 0, row_sets[0])
    gather_rows((parts[2], parts[3], *parts[4:]), 1, row_sets[1])
    for i, (side, part, copy) in enumerate(steps):
        copy.wait()
        if i + 2 < len(steps):
            steps[i + 2][2].start()
        outs[side][:, part] = SCALE * lax.dot_general(
            row_sets[side][...],
            held[side, part, :],
            (((1,), (1,)), ((), ())),
            preferred_element_type=jnp.float32,
        )


STEP = 512
NEAR = ((0, 1, 7, 2, 6), (0, 1, 7, 2, 6))
FAR = ((5, 3, 4), (3, 5, 4))


def local(amplitudes, integral_tiles, tile_rows, tile_cols, mirror, occupied_sum, virtual_sum):
    local_rows, total_width = amplitudes.shape
    width = integral_tiles.shape[1]
    blocks = total_width // width
    half = local_rows // 2
    kind = amplitudes.dtype
    here = lax.axis_index("tile")

    def hits_at(dz):
        plane = jnp.stack([at_plane(here, dz) ^ bit for bit in BITS])
        named = plane[:, None] == jnp.arange(tile_rows.shape[0], dtype=jnp.int32)[None, :]
        outs = jnp.sum(jnp.where(named, tile_rows[None, :], 0), axis=1)
        hits = outs[None, :] == jnp.arange(blocks, dtype=jnp.int32)[:, None]
        return hits.astype(jnp.float32)

    def spread(hits, four):
        total = sum(
            hits[:, i][:, None, None] * f.astype(jnp.float32)[None] for i, f in enumerate(four)
        )
        return total.reshape(blocks * half, width)

    def shape(*dims):
        return jax.ShapeDtypeStruct((*dims, width), kind)

    def trimmed(up, down):
        return call(trim_kernel, [shape(4, half)] * 2, (tile_cols, up, down), smem=1)

    core_tile = send(integral_tiles[0], core=1)
    blocked = amplitudes.reshape(local_rows, blocks, width).transpose(1, 0, 2)
    halves = [blocked[:, :half], blocked[:, half:]]
    pieces = [[None] * 8, [None] * 8]
    pieces[0][0], pieces[1][0] = halves

    def gathered(up, down):
        size = up.shape
        flat = [a.reshape(size[0] * size[1], width) for a in (up, down)]
        arrived = tied(send(flat[0], dz=1), send(flat[1], dz=-1))
        return [a.reshape(size) for a in arrived]

    long = halves
    short = [halves[1], halves[0]]
    for hop in range(1, 5):
        long = gathered(*(long if hop < 4 else trimmed(*long)))
        pieces[0][-hop % 8], pieces[1][hop] = long
        if hop < 4:
            short = gathered(*(short if hop < 3 else trimmed(*short)))
            pieces[1][-hop % 8], pieces[0][hop] = short

    def collected(deltas):
        return [pieces[h][d] for h in range(2) for d in deltas[h]]

    def crossed(parts):
        own, cross, up, down = [a.reshape(2, -1, width) for a in parts]
        own, cross = [a.reshape(-1, width) for a in (own, cross)]
        return own, cross, send(up, dy=1), send(down, dy=-1)

    count = len(NEAR[0])
    near = crossed(
        call(
            functools.partial(pick_kernel, count),
            [shape(2, count, half)] * 4,
            (tile_cols, *collected(NEAR)),
            smem=1,
        )
    )
    far = crossed(call(far_kernel, [shape(2, 3, half)] * 4, (tile_cols, *collected(FAR)), smem=1))
    sides = (*near[2:], *far[2:])
    per_core = local_rows * 16
    tile = integral_tiles[0]
    mine, other = call(
        terms_kernel,
        [jax.ShapeDtypeStruct((per_core, width), jnp.float32)] * 2,
        (near[0], far[0], near[1], far[1], *sides, tile, core_tile),
        scratch=[
            pltpu.VMEM((per_core, width), kind),
            pltpu.VMEM((per_core, width), kind),
            pltpu.VMEM((2, width, width), kind),
            pltpu.SemaphoreType.DMA((2 * pl.cdiv(width, STEP),)),
        ],
        flops=4 * per_core * width * width,
        moved=4 * width * width,
        far=2,
        limit=44,
    )
    mine, other = mine.astype(jnp.float16), other.astype(jnp.float16)

    def back_by_y(at, size):
        below, above = [
            jnp.stack([array[start : start + size] for array in (mine, other)])
            for start in (at, at + size)
        ]
        return send(below, dy=-1), send(above, dy=1)

    near_size, far_size = count * half, 3 * half
    sides_at = 2 * (near_size + far_size)
    far_back = back_by_y(sides_at + 2 * near_size, far_size)
    near_back = back_by_y(sides_at, near_size)

    def planes(deltas, at, back):
        four = {}
        for h in range(2):
            size = len(deltas[h]) * half
            parts = [array[at + h * size : at + (h + 1) * size] for array in (mine, other)]
            parts += [back[h][0], back[h][1]]
            for i, delta in enumerate(deltas[h]):
                four[h, delta] = [part[i * half : (i + 1) * half] for part in parts]
        return four

    four = planes(FAR, 2 * near_size, far_back)
    raw = {
        key: jnp.concatenate(four.pop(key), axis=0) for key in ((0, 4), (1, 4), (1, 5), (0, 3))
    }
    above_hits, my_hits, below_hits = [hits_at(dz) for dz in (1, 0, -1)]

    def passed_on(below, above):
        below, above = [a.astype(jnp.float16) for a in (below, above)]
        return tied(send(below, dz=-1), send(above, dz=1))

    def first_hop(below, above):
        arrived = passed_on(below, above)
        return [
            spread(hits, jnp.split(a, 4)) for hits, a in zip((above_hits, below_hits), arrived)
        ]

    def hop_on(below, above):
        return [a.astype(jnp.float32) for a in passed_on(below, above)]

    long = first_hop(raw[0, 4], raw[1, 4])
    short = first_hop(raw[1, 5], raw[0, 3])
    dense = dict(zip(four, tied(*[spread(my_hits, f) for f in four.values()])))
    *near_back, long[0], long[1] = tied(*near_back, *long)
    four = planes(NEAR, 0, near_back)
    dense.update(zip(four, tied(*[spread(my_hits, f) for f in four.values()])))
    for hop in range(3, 0, -1):
        long = hop_on(long[0] + dense[0, 8 - hop], long[1] + dense[1, hop])
        if hop < 3:
            short = hop_on(short[0] + dense[1, 8 - hop], short[1] + dense[0, hop])
    sums = [long[0] + short[1], long[1] + short[0]]
    residual = jnp.concatenate(
        [(sums[h] + dense[h, 0]).reshape(blocks, half, width) for h in range(2)], axis=1
    ) * (1.0 / SCALE)
    residual = residual.transpose(1, 0, 2).reshape(local_rows, total_width)
    partner_rows = send(residual.astype(jnp.bfloat16), dy=2).astype(residual.dtype)
    partner_index = mirror % local_rows
    combined = residual - 0.5 * partner_rows[partner_index]
    denominator = virtual_sum[None, :] - occupied_sum[:, None]
    return amplitudes.astype(jnp.float32) + combined / denominator


def solution(mesh):
    in_specs = (
        P(("pair", "tile"), None),
        P("tile", None, None),
        P(),
        P(),
        P(("pair", "tile")),
        P(("pair", "tile")),
        P(),
    )
    out_specs = P(("pair", "tile"), None)
    return jax.shard_map(local, mesh=mesh, in_specs=in_specs, out_specs=out_specs, check_vma=False)
```

```python
import functools

import jax
import jax.numpy as jnp
from jax import lax
from jax.experimental import pallas as pl
from jax.experimental.pallas import tpu as pltpu
from jax.sharding import PartitionSpec as P

BOTH = ("pair", "tile")
SCALE = 8.0


def moved(dx=0, dy=0, dz=0, core=0):
    pairs = []
    for x in range(4):
        for y in range(4):
            for z in range(8):
                for c in range(2):
                    far_y = (y + dy) % 4
                    here = ((y // 2) * 4 + x) * 32 + (y % 2) * 16 + z * 2 + c
                    there = (
                        ((far_y // 2) * 4 + (x + dx) % 4) * 32
                        + (far_y % 2) * 16
                        + ((z + dz) % 8) * 2
                        + (c ^ core)
                    )
                    pairs.append((here, there))
    return pairs


def send(array, **by):
    return lax.ppermute(array, BOTH, moved(**by))


def tied(*arrays):
    return lax.optimization_barrier(arrays)


def vmem():
    return pl.BlockSpec(memory_space=pltpu.VMEM)


def call(kernel, outs, operands, smem=0, scratch=(), flops=0, moved=None, far=0, limit=24):
    if moved is None:
        moved = sum(2 * out.size * out.dtype.itemsize for out in outs)
    specs = [pl.BlockSpec(memory_space=pltpu.SMEM)] * smem + [vmem()] * (len(operands) - smem - far)
    specs += [pl.BlockSpec(memory_space=pltpu.HBM)] * far
    return pl.pallas_call(
        kernel,
        out_shape=list(outs),
        in_specs=specs,
        out_specs=[vmem()] * len(outs),
        scratch_shapes=list(scratch),
        cost_estimate=pl.CostEstimate(flops=flops, bytes_accessed=moved, transcendentals=0),
        compiler_params=pltpu.CompilerParams(vmem_limit_bytes=limit * 1024 * 1024),
    )(*operands)


BITS = (0, 1, 16, 17)


def at_plane(here, dz):
    return (here & 17) | ((((here >> 1) + dz) & 7) << 1)


def pick_kernel(count, cols_ref, *refs):
    low, high = refs[:count], refs[count : 2 * count]
    own_ref, cross_ref, up_ref, down_ref = refs[2 * count :]
    here = lax.axis_index("tile")
    mine, core, far, far_core = [cols_ref[here ^ bit] for bit in BITS]
    for i in range(count):
        own_ref[0, i] = low[i][mine]
        own_ref[1, i] = high[i][mine]
        cross_ref[0, i] = low[i][core]
        cross_ref[1, i] = high[i][core]
        up_ref[0, i] = low[i][far]
        up_ref[1, i] = low[i][far_core]
        down_ref[0, i] = high[i][far]
        down_ref[1, i] = high[i][far_core]


def trim_kernel(cols_ref, up_ref, down_ref, to_up_ref, to_down_ref):
    here = lax.axis_index("tile")
    for dz, source, target in ((1, up_ref, to_up_ref), (-1, down_ref, to_down_ref)):
        for j, bit in enumerate(BITS):
            target[j] = source[cols_ref[at_plane(here, dz) ^ bit]]


def far_kernel(cols_ref, *refs):
    low, high = refs[:3], refs[3:6]
    own_ref, cross_ref, up_ref, down_ref = refs[6:]
    here = lax.axis_index("tile")
    for i in range(3):
        four = [cols_ref[here ^ bit] for bit in BITS] if i == 0 else range(4)
        own_ref[0, i] = low[i][four[0]]
        own_ref[1, i] = high[i][four[0]]
        cross_ref[0, i] = low[i][four[1]]
        cross_ref[1, i] = high[i][four[1]]
        for s in range(2):
            up_ref[s, i] = low[i][four[2 + s]]
            down_ref[s, i] = high[i][four[2 + s]]


def gather_rows(parts, side, rows_ref):
    at = 0
    for part in parts:
        value = part[...] if len(part.shape) == 2 else part[side]
        rows_ref[at : at + value.shape[0]] = value
        at += value.shape[0]


def terms_kernel(*refs):
    parts, tiles = refs[:8], refs[8:10]
    outs, row_sets, held, sems = refs[10:12], refs[12:14], refs[14], refs[15]
    width = tiles[0].shape[0]
    steps = []
    for side in range(2):
        for start in range(0, width, STEP):
            part = slice(start, min(start + STEP, width))
            copy = pltpu.make_async_copy(
                tiles[side].at[part], held.at[side, part], sems.at[len(steps)]
            )
            steps.append((side, part, copy))
    for _, _, copy in steps[:2]:
        copy.start()
    gather_rows((parts[0], parts[1], *parts[4:]), 0, row_sets[0])
    gather_rows((parts[2], parts[3], *parts[4:]), 1, row_sets[1])
    for i, (side, part, copy) in enumerate(steps):
        copy.wait()
        if i + 2 < len(steps):
            steps[i + 2][2].start()
        outs[side][:, part] = SCALE * lax.dot_general(
            row_sets[side][...],
            held[side, part, :],
            (((1,), (1,)), ((), ())),
            preferred_element_type=jnp.float32,
        )


STEP = 512
NEAR = ((0, 1, 7, 2, 6), (0, 1, 7, 2, 6))
FAR = ((5, 3, 4), (3, 5, 4))


def local(amplitudes, integral_tiles, tile_rows, tile_cols, mirror, occupied_sum, virtual_sum):
    local_rows, total_width = amplitudes.shape
    width = integral_tiles.shape[1]
    blocks = total_width // width
    half = local_rows // 2
    kind = amplitudes.dtype
    here = lax.axis_index("tile")

    def hits_at(dz):
        plane = jnp.stack([at_plane(here, dz) ^ bit for bit in BITS])
        named = plane[:, None] == jnp.arange(tile_rows.shape[0], dtype=jnp.int32)[None, :]
        outs = jnp.sum(jnp.where(named, tile_rows[None, :], 0), axis=1)
        hits = outs[None, :] == jnp.arange(blocks, dtype=jnp.int32)[:, None]
        return hits.astype(jnp.float32)

    def spread(hits, four):
        total = sum(
            hits[:, i][:, None, None] * f.astype(jnp.float32)[None] for i, f in enumerate(four)
        )
        return total.reshape(blocks * half, width)

    def shape(*dims):
        return jax.ShapeDtypeStruct((*dims, width), kind)

    def trimmed(up, down):
        return call(trim_kernel, [shape(4, half)] * 2, (tile_cols, up, down), smem=1)

    core_tile = send(integral_tiles[0], core=1)
    blocked = amplitudes.reshape(local_rows, blocks, width).transpose(1, 0, 2)
    halves = [blocked[:, :half], blocked[:, half:]]
    pieces = [[None] * 8, [None] * 8]
    pieces[0][0], pieces[1][0] = halves

    def gathered(up, down):
        size = up.shape
        flat = [a.reshape(size[0] * size[1], width) for a in (up, down)]
        arrived = tied(send(flat[0], dz=1), send(flat[1], dz=-1))
        return [a.reshape(size) for a in arrived]

    def collected(deltas):
        return [pieces[h][d] for h in range(2) for d in deltas[h]]

    count = len(NEAR[0])
    long = halves
    short = [halves[1], halves[0]]
    for hop in range(1, 5):
        if hop == 4:
            *near_parts, long[0], long[1] = tied(*near_parts, *long)
        long = gathered(*(long if hop < 4 else trimmed(*long)))
        pieces[0][-hop % 8], pieces[1][hop] = long
        if hop < 4:
            short = gathered(*(short if hop < 3 else trimmed(*short)))
            pieces[1][-hop % 8], pieces[0][hop] = short
        if hop == 2:
            near_parts = call(
                functools.partial(pick_kernel, count),
                [shape(2, count, half)] * 4,
                (tile_cols, *collected(NEAR)),
                smem=1,
            )

    def crossed(parts):
        own, cross, up, down = [a.reshape(2, -1, width) for a in parts]
        own, cross = [a.reshape(-1, width) for a in (own, cross)]
        return own, cross, send(up, dy=1), send(down, dy=-1)

    near = crossed(near_parts)
    far = crossed(call(far_kernel, [shape(2, 3, half)] * 4, (tile_cols, *collected(FAR)), smem=1))
    sides = (*near[2:], *far[2:])
    per_core = local_rows * 16
    tile = integral_tiles[0]
    mine, other = call(
        terms_kernel,
        [jax.ShapeDtypeStruct((per_core, width), jnp.float32)] * 2,
        (near[0], far[0], near[1], far[1], *sides, tile, core_tile),
        scratch=[
            pltpu.VMEM((per_core, width), kind),
            pltpu.VMEM((per_core, width), kind),
            pltpu.VMEM((2, width, width), kind),
            pltpu.SemaphoreType.DMA((2 * pl.cdiv(width, STEP),)),
        ],
        flops=4 * per_core * width * width,
        moved=4 * width * width,
        far=2,
        limit=44,
    )
    mine, other = mine.astype(jnp.float16), other.astype(jnp.float16)

    def back_by_y(at, size):
        below, above = [
            jnp.stack([array[start : start + size] for array in (mine, other)])
            for start in (at, at + size)
        ]
        return send(below, dy=-1), send(above, dy=1)

    near_size, far_size = count * half, 3 * half
    sides_at = 2 * (near_size + far_size)
    far_back = back_by_y(sides_at + 2 * near_size, far_size)
    near_back = back_by_y(sides_at, near_size)

    def planes(deltas, at, back):
        four = {}
        for h in range(2):
            size = len(deltas[h]) * half
            parts = [array[at + h * size : at + (h + 1) * size] for array in (mine, other)]
            parts += [back[h][0], back[h][1]]
            for i, delta in enumerate(deltas[h]):
                four[h, delta] = [part[i * half : (i + 1) * half] for part in parts]
        return four

    four = planes(FAR, 2 * near_size, far_back)
    raw = {
        key: jnp.concatenate(four.pop(key), axis=0) for key in ((0, 4), (1, 4), (1, 5), (0, 3))
    }
    above_hits, my_hits, below_hits = [hits_at(dz) for dz in (1, 0, -1)]

    def passed_on(below, above):
        below, above = [a.astype(jnp.float16) for a in (below, above)]
        return tied(send(below, dz=-1), send(above, dz=1))

    def first_hop(below, above):
        arrived = passed_on(below, above)
        return [
            spread(hits, jnp.split(a, 4)) for hits, a in zip((above_hits, below_hits), arrived)
        ]

    def hop_on(below, above):
        return [a.astype(jnp.float32) for a in passed_on(below, above)]

    long = first_hop(raw[0, 4], raw[1, 4])
    short = first_hop(raw[1, 5], raw[0, 3])
    dense = dict(zip(four, tied(*[spread(my_hits, f) for f in four.values()])))
    *near_back, long[0], long[1] = tied(*near_back, *long)
    four = planes(NEAR, 0, near_back)
    dense.update(zip(four, tied(*[spread(my_hits, f) for f in four.values()])))
    for hop in range(3, 0, -1):
        long = hop_on(long[0] + dense[0, 8 - hop], long[1] + dense[1, hop])
        if hop < 3:
            short = hop_on(short[0] + dense[1, 8 - hop], short[1] + dense[0, hop])
    sums = [long[0] + short[1], long[1] + short[0]]
    residual = jnp.concatenate(
        [(sums[h] + dense[h, 0]).reshape(blocks, half, width) for h in range(2)], axis=1
    ) * (1.0 / SCALE)
    residual = residual.transpose(1, 0, 2).reshape(local_rows, total_width)
    partner_rows = send(residual.astype(jnp.bfloat16), dy=2).astype(residual.dtype)
    partner_index = mirror % local_rows
    combined = residual - 0.5 * partner_rows[partner_index]
    denominator = virtual_sum[None, :] - occupied_sum[:, None]
    return amplitudes.astype(jnp.float32) + combined / denominator


def solution(mesh):
    in_specs = (
        P(("pair", "tile"), None),
        P("tile", None, None),
        P(),
        P(),
        P(("pair", "tile")),
        P(("pair", "tile")),
        P(),
    )
    out_specs = P(("pair", "tile"), None)
    return jax.shard_map(local, mesh=mesh, in_specs=in_specs, out_specs=out_specs, check_vma=False)
```
